512 devices in a mesh: row: 16 (over z_lo, x), col: 8 (over z_hi, core), vis: 4 (over y).
Axes of the slice: x: 4, y: 4, z: 16 (z_hi: 4, z_lo: 4; z = z_hi * 4 + z_lo), core: 2. Of those that a mesh axis runs over, the one named last changes fastest.
Arguments:
- tile_rows: bfloat16 [2048, 12800], P('vis', 'row'), may hold values from -6 to 6
- tile_slot: int32 [4], replicated, may hold values from 0 to 7, as said below
- proj_weight: bfloat16 [12800, 8192], P('row', ('col', 'vis')), may hold values from -0.0546875 to 0.0546875
- gate_weight: bfloat16 [8192, 14784], P('col', ('row', 'vis')), may hold values from -0.0625 to 0.0625
- up_weight: bfloat16 [8192, 14784], P('col', ('row', 'vis')), may hold values from -0.0625 to 0.0625
- cotangent: bfloat16 [1024, 14784], P('vis', 'row'), may hold values from -0.19921875 to 0.19921875
Outputs:
- proj_grad: bfloat16 [12800, 8192], P('row', ('col', 'vis'))
The draws below stay inside these ranges and needn't reach their ends.
Inputs may be any that keep to these rules, and one draw needn't show every extreme that they name: `tile_slot`: the entries are distinct slots of the 8 slots; in every draw all 2 slots of some vision group are used.
All inputs are finite; a program needn't handle non-finite values.
Results may differ from the reference program's by a relative error of at most 0.01.
Values may be sent and summed in bfloat16 or wider, within the bound.
No kernel may reach another device: no remote copies, remote signals or barrier semaphores. Data moves between devices by JAX's collectives and lax.ppermute only.
A program may use at most 64 MiB of HBM per device.

```python
import jax
import jax.numpy as jnp
from jax import lax

DV = 12800
DM = 8192
FFW = 14784
TILE = 256
CAPT = 2
TILES = 4
TOKENS = 1024
N_VIS = 4


def draw_tile_slot(key, part):
    slot_count = N_VIS * CAPT
    key = jax.random.fold_in(jax.random.fold_in(key, 11), part)
    first_key = jax.random.fold_in(key, 21)
    second_key = jax.random.fold_in(key, 22)
    third_key = jax.random.fold_in(key, 23)
    full_group = jax.random.randint(first_key, (), 0, N_VIS)
    shuffled = jax.random.permutation(second_key, slot_count)
    owner = shuffled // CAPT
    at_end = jnp.logical_or(shuffled == 0, shuffled == slot_count - 1)
    rank = jnp.where(owner == full_group, 0, jnp.where(at_end, 1, 2))
    score = rank * slot_count + jnp.arange(slot_count)
    order = jnp.argsort(score, stable=True)
    chosen = shuffled[order][:TILES]
    return chosen[jax.random.permutation(third_key, TILES)].astype(jnp.int32)


def block_scale(own_key, shape, split, low, top_value):
    level = 1.0
    for dim, blocks in split:
        heights = jax.random.uniform(jax.random.fold_in(jax.random.fold_in(own_key, 6), dim), (blocks,), jnp.float32, low / len(split), top_value / len(split))
        level = level * jnp.repeat(jnp.exp(heights), shape[dim] // blocks).reshape((-1,) + (1,) * (len(shape) - 1 - dim))
    return level


def gaussian(key, shape, spread, limit, cuts=(), dtype=jnp.bfloat16):
    entries = spread * jax.random.normal(key, shape, jnp.float32)
    if cuts:
        entries = entries * block_scale(key, shape, cuts, -0.22, 0.18)
    return jnp.clip(entries, -limit, limit).astype(dtype)


def setup_inputs(seed: int = 0) -> dict:
    keys = jax.random.split(jax.random.key(seed), 7)
    return {
        "tile_rows": gaussian(keys[0], (N_VIS * CAPT * TILE, DV), 1.0, 6.0, ((0, 4), (1, 16))),
        "tile_slot": draw_tile_slot(jax.random.fold_in(keys[6], 71), 0),
        "proj_weight": gaussian(keys[2], (DV, DM), DV ** -0.5, 0.0546875, ((0, 16), (1, 32))),
        "gate_weight": gaussian(keys[3], (DM, FFW), DM ** -0.5, 0.0625, ((0, 8), (1, 64))),
        "up_weight": gaussian(keys[4], (DM, FFW), DM ** -0.5, 0.0625, ((0, 8), (1, 64))),
        "cotangent": gaussian(keys[5], (TOKENS, FFW), 0.03, 0.19921875, ((0, 4), (1, 16))),
    }


def gelu_exact(value):
    return 0.5 * value * (1.0 + lax.erf(value * 0.7071067811865476))


def gelu_slope(value):
    normal_cdf = 0.5 * (1.0 + lax.erf(value * 0.7071067811865476))
    return normal_cdf + value * jnp.exp(-0.5 * value * value) * 0.3989422804014327


def reference(tile_rows, tile_slot, proj_weight, gate_weight, up_weight, cotangent):
    tokens = tile_rows.reshape(N_VIS * CAPT, TILE, DV)[tile_slot].reshape(TILES * TILE, DV)
    preact = jnp.dot(tokens, proj_weight, preferred_element_type=jnp.float32)
    hidden = gelu_exact(preact).astype(jnp.bfloat16)
    gate_sum = jnp.dot(hidden, gate_weight, preferred_element_type=jnp.float32)
    up_sum = jnp.dot(hidden, up_weight, preferred_element_type=jnp.float32)
    sigmoid_gate = jax.nn.sigmoid(gate_sum)
    d_gate = (cotangent * up_sum * sigmoid_gate * (1.0 + gate_sum * (1.0 - sigmoid_gate))).astype(jnp.bfloat16)
    d_up = (cotangent * gate_sum * sigmoid_gate).astype(jnp.bfloat16)
    dact = jnp.dot(d_gate, gate_weight.T, preferred_element_type=jnp.float32)
    dact = dact + jnp.dot(d_up, up_weight.T, preferred_element_type=jnp.float32)
    dpre = (dact * gelu_slope(preact)).astype(jnp.bfloat16)
    return jnp.dot(tokens.T, dpre, preferred_element_type=jnp.float32).astype(jnp.bfloat16)
```

```python
import jax
import jax.numpy as jnp
from jax import lax
from jax.sharding import PartitionSpec as P

TILE = 256
F32 = jnp.float32
BF16 = jnp.bfloat16


def gelu_exact(value):
    return 0.5 * value * (1.0 + lax.erf(value * 0.7071067811865476))


def gelu_slope(value):
    normal_cdf = 0.5 * (1.0 + lax.erf(value * 0.7071067811865476))
    return normal_cdf + value * jnp.exp(-0.5 * value * value) * 0.3989422804014327


def dot(a, b, contract):
    return lax.dot_general(a, b, (contract, ((), ())), preferred_element_type=F32)


def shards(tile_rows, tile_slot, proj_weight, gate_weight, up_weight, cotangent):
    n_vis, n_row, n_col = lax.axis_size("vis"), lax.axis_size("row"), lax.axis_size("col")
    n_quarter = n_col // 2
    vis, col = lax.axis_index("vis"), lax.axis_index("col")
    core, quarter = col % 2, col // 2
    features = tile_rows.shape[1]
    half = features // 2
    core_pairs = [(2 * i + k, 2 * i + 1 - k) for i in range(n_quarter) for k in range(2)]
    quarter_groups = [[2 * i + k for i in range(n_quarter)] for k in range(2)]
    n_tiles = tile_slot.shape[0]
    slots = tile_rows.shape[0] // TILE

    gate_t, up_t = gate_weight.T, up_weight.T
    gate_block = lax.all_gather(gate_t, "vis", axis=0)
    up_block = lax.all_gather(up_t, "vis", axis=0)

    rows_t = tile_rows.T
    own_half = lax.dynamic_slice_in_dim(rows_t, core * half, half, 0)
    arrived = lax.all_to_all(jnp.broadcast_to(own_half[None], (n_vis,) + own_half.shape), "vis", 0, 0)
    picked = []
    for t in range(n_tiles):
        slot = tile_slot[t]
        picked.append(
            lax.dynamic_slice(arrived, (slot // slots, 0, (slot % slots) * TILE), (1, half, TILE))[0]
        )
    mine = jnp.concatenate(picked, axis=1)
    other = lax.ppermute(mine, "col", core_pairs)
    first = jnp.where(core == 0, mine, other)
    second = jnp.where(core == 0, other, mine)
    tokens_t = jnp.concatenate([first, second], axis=0)

    partial = dot(tokens_t, proj_weight, ((0,), (0,))).astype(BF16)
    n_tok, width = partial.shape
    share = n_tok // (n_vis * n_row)
    partial = lax.all_to_all(partial.reshape(n_vis * n_row, share, width), ("vis", "row"), 0, 0)
    preact = jnp.sum(partial.reshape(n_vis, n_row, share, width).astype(F32), axis=1)
    preact = jnp.transpose(preact, (1, 0, 2)).reshape(share, n_vis * width)
    hidden = gelu_exact(preact).astype(BF16)
    slope = gelu_slope(preact)
    hidden = lax.all_to_all(jnp.broadcast_to(hidden[None], (n_row,) + hidden.shape), "row", 0, 0)
    hidden = hidden.reshape(TILE, n_vis * width)

    parts = []
    for block in (gate_block, up_block):
        parts.append(jnp.stack([dot(block[k], hidden, ((1,), (1,))) for k in range(n_vis)]))
    both = jnp.stack(parts, axis=1)
    lane = TILE // 2
    keep = lax.dynamic_slice_in_dim(both, core * lane, lane, 3)
    give = lax.dynamic_slice_in_dim(both, (1 - core) * lane, lane, 3).astype(BF16)
    got = lax.ppermute(give, "col", core_pairs)
    pair_sum = (keep + got.astype(F32)).astype(BF16)
    pieces = lax.all_to_all(pair_sum, "col", 0, 0, axis_index_groups=quarter_groups)
    gate_sum, up_sum = jnp.sum(pieces.astype(F32), axis=0)

    unit = gate_t.shape[0]
    cot = lax.dynamic_slice(cotangent.T, (quarter * unit, core * lane), (unit, lane)).astype(F32)
    sig = jax.nn.sigmoid(gate_sum)
    d_gate = (cot * up_sum * sig * (1.0 + gate_sum * (1.0 - sig))).astype(BF16)
    d_up = (cot * gate_sum * sig).astype(BF16)
    d_both = jnp.stack([d_gate, d_up])
    d_all = lax.all_to_all(
        jnp.broadcast_to(d_both[None], (n_quarter,) + d_both.shape), "col", 0, 0,
        axis_index_groups=quarter_groups,
    )
    d_other = lax.ppermute(d_all, "col", core_pairs)
    d_first = jnp.where(core == 0, d_all, d_other)
    d_second = jnp.where(core == 0, d_other, d_all)
    d_all = jnp.concatenate([d_first, d_second], axis=3)

    dact = 0.0
    for k in range(n_vis):
        dact = dact + dot(d_all[k, 0], gate_block[k], ((0,), (0,)))
        dact = dact + dot(d_all[k, 1], up_block[k], ((0,), (0,)))
    dact = dact.astype(BF16).reshape(n_row, share, n_vis * width)
    dact = lax.all_to_all(dact, "row", 0, 0)
    dact = jnp.sum(dact.astype(F32), axis=0)
    dpre = (dact * slope).astype(BF16)
    dpre = jnp.transpose(dpre.reshape(share, n_vis, width), (1, 0, 2))
    dpre = jnp.broadcast_to(dpre[:, None], (n_vis, n_row, share, width))
    dpre = lax.all_to_all(dpre.reshape(n_vis * n_row, share, width), ("vis", "row"), 0, 0)
    dpre = dpre.reshape(n_tok, width)
    return dot(tokens_t, dpre, ((1,), (0,))).astype(BF16)


def solution(mesh):
    in_specs = (
        P("vis", "row"),
        P(),
        P("row", ("col", "vis")),
        P("col", ("row", "vis")),
        P("col", ("row", "vis")),
        P("vis", "row"),
    )
    out_specs = P("row", ("col", "vis"))
    return jax.shard_map(shards, mesh=mesh, in_specs=in_specs, out_specs=out_specs, check_vma=False)
```

```python
import jax
import jax.numpy as jnp
from jax import lax
from jax.experimental import pallas as pl
from jax.experimental.pallas import tpu as pltpu
from jax.sharding import PartitionSpec as P

TILE = 256
F32 = jnp.float32
BF16 = jnp.bfloat16


def gelu_exact(value):
    return 0.5 * value * (1.0 + lax.erf(value * 0.7071067811865476))


def gelu_slope(value):
    normal_cdf = 0.5 * (1.0 + lax.erf(value * 0.7071067811865476))
    return normal_cdf + value * jnp.exp(-0.5 * value * value) * 0.3989422804014327


def dot(a, b, contract):
    return lax.dot_general(a, b, (contract, ((), ())), preferred_element_type=F32)


def pick_kernel(slot_ref, arrived_ref, out_ref):
    out_ref[...] = arrived_ref[0]


def pick_tiles(tile_slot, arrived, slots):
    _, rows, _ = arrived.shape
    tiles = tile_slot.shape[0]
    return pl.pallas_call(
        pick_kernel,
        grid_spec=pltpu.PrefetchScalarGridSpec(
            num_scalar_prefetch=1,
            grid=(tiles,),
            in_specs=[
                pl.BlockSpec((1, rows, TILE), lambda t, slot: (slot[t] // slots, 0, slot[t] % slots))
            ],
            out_specs=pl.BlockSpec((rows, TILE), lambda t, slot: (0, t)),
        ),
        out_shape=jax.ShapeDtypeStruct((rows, tiles * TILE), BF16),
        cost_estimate=pl.CostEstimate(flops=0, bytes_accessed=4 * rows * tiles * TILE, transcendentals=0),
    )(tile_slot, arrived)


def weight_copies(weights, held, sems):
    return [pltpu.make_async_copy(w, b, sems.at[i]) for i, (w, b) in enumerate(zip(weights, held))]


def gate_body(place_ref, h_ref, weights, out_ref, held, sems):
    n = len(weights) // 2
    copies = weight_copies(weights, held, sems)
    for i in range(n):
        copies[i].start()
        copies[i + n].start()
    core, blocks, rows = place_ref[0], out_ref.shape[0], out_ref.shape[1]
    block, at = 0, 0
    for i in range(n):
        size = held[i].shape[0]
        copies[i].wait()
        total = dot(held[i][...], h_ref[core], ((1,), (1,)))
        copies[i + n].wait()
        total = total + dot(held[i + n][...], h_ref[1 - core], ((1,), (1,)))
        chunk = (block + blocks - place_ref[1]) % blocks
        out_ref[chunk, at : at + size, :] = total.astype(BF16)
        at += size
        block, at = block + at // rows, at % rows


def dact_body(place_ref, d_ref, weights, out_ref, held, sems):
    n = len(weights) // 2
    copies = weight_copies(weights, held, sems)
    for copy in copies:
        copy.start()
    core, blocks, rows = place_ref[0], d_ref.shape[0], d_ref.shape[1]
    step = 256
    for j in range(2):
        for i in range(n):
            copies[j * n + i].wait()
        slot = core if j == 0 else 1 - core
        for c in range(0, out_ref.shape[2], step):
            total, block, at = None, 0, 0
            for i in range(n):
                w = held[j * n + i]
                size = w.shape[0]
                chunk = (block + blocks - place_ref[1]) % blocks
                term = dot(d_ref[chunk, at : at + size, :], w[:, c : c + step], ((0,), (0,)))
                total = term if total is None else total + term
                at += size
                block, at = block + at // rows, at % rows
            out_ref[slot, :, c : c + step] = total.astype(BF16)


def with_weights(body, place, operand, weights, out_shape, flops):
    n = len(weights)

    def kernel(place_ref, operand_ref, *refs):
        body(place_ref, operand_ref, refs[:n], refs[n], refs[n + 1 : -1], refs[-1])

    moved = sum(w.size for w in weights) + operand.size
    return pl.pallas_call(
        kernel,
        in_specs=[pl.BlockSpec(memory_space=pltpu.SMEM), pl.BlockSpec(memory_space=pltpu.VMEM)]
        + [pl.BlockSpec(memory_space=pl.ANY)] * n,
        out_specs=pl.BlockSpec(memory_space=pltpu.VMEM),
        out_shape=jax.ShapeDtypeStruct(out_shape, BF16),
        scratch_shapes=[pltpu.VMEM(w.shape, BF16) for w in weights] + [pltpu.SemaphoreType.DMA((n,))],
        compiler_params=pltpu.CompilerParams(vmem_limit_bytes=60 * 2**20),
        cost_estimate=pl.CostEstimate(flops=flops, bytes_accessed=2 * moved, transcendentals=0),
    )(place, operand, *weights)


def shards(tile_rows, tile_slot, proj_weight, gate_weight, up_weight, cotangent):
    n_vis, n_row, n_col = lax.axis_size("vis"), lax.axis_size("row"), lax.axis_size("col")
    n_x = tile_slot.shape[0]
    n_low = n_row // n_x
    n_quarter = n_col // 2
    row, col, vis = lax.axis_index("row"), lax.axis_index("col"), lax.axis_index("vis")
    core, quarter, x = col % 2, col // 2, row % n_x
    features = tile_rows.shape[1]
    half = features // 2
    slots = tile_rows.shape[0] // TILE
    core_pairs = [(2 * i + k, 2 * i + 1 - k) for i in range(n_quarter) for k in range(2)]
    quarter_groups = [[2 * i + k for i in range(n_quarter)] for k in range(2)]
    sheet_groups = [
        [(low * n_x + i) * n_vis + v for i in range(n_x) for low in range(n_low) for v in range(n_vis)]
    ]
    column_groups = [
        [
            ((low * n_x + i) * n_col + 2 * q + k) * n_vis + v
            for k in range(2)
            for low in range(n_low)
            for v in range(n_vis)
        ]
        for i in range(n_x)
        for q in range(n_quarter)
    ]
    shifts = [0, 1, 3, 2]

    rows_t = tile_rows.T
    own_half = lax.dynamic_slice_in_dim(rows_t, core * half, half, 0)
    own_half = jnp.broadcast_to(own_half[None], (n_vis,) + own_half.shape)

    unit = gate_weight.shape[1]
    pad = -unit % 8
    weights = jnp.stack([gate_weight.T, up_weight.T])
    weights = jnp.pad(weights, ((0, 0), (0, pad), (0, 0))).reshape(2 * (unit + pad), -1)

    def from_x(value, shift):
        pairs = [
            (low * n_x + i, low * n_x + (i - shift) % n_x) for low in range(n_low) for i in range(n_x)
        ]
        return lax.ppermute(value, "row", pairs)

    def from_core(value):
        return lax.ppermute(value, "col", core_pairs)

    arrived = lax.all_to_all(own_half, "vis", 0, 0)
    right, left, weights_o = from_x(weights, 1), from_x(weights, -1), from_core(weights)
    mine = pick_tiles(tile_slot, arrived, slots)
    other = from_core(mine)
    other, right, left, weights_o = lax.optimization_barrier((other, right, left, weights_o))
    far_gate, far_up = right[: unit + pad], left[unit + pad :]
    first = jnp.where(core == 0, mine, other)
    second = jnp.where(core == 0, other, mine)
    tokens_t = jnp.concatenate([first, second], axis=0)

    partial = dot(tokens_t, proj_weight, ((0,), (0,))).astype(BF16)
    n_tok, width = partial.shape
    spread = n_low * n_vis
    share = TILE // spread
    few = share // 2
    lane = TILE // 2
    model = n_vis * width
    partial = jnp.transpose(partial.reshape(n_x, 2, spread, few, width), (0, 2, 1, 3, 4))
    partial = partial.reshape(n_x * spread, share, width)
    partial = lax.all_to_all(partial, ("row", "vis"), 0, 0, axis_index_groups=sheet_groups)
    far_gate, far_up = from_x(far_gate, 1), from_x(far_up, -1)
    partial, far_gate, far_up = lax.optimization_barrier((partial, far_gate, far_up))
    preact = jnp.sum(partial.reshape(n_row, n_vis, share, width).astype(F32), axis=0)
    preact = jnp.transpose(preact, (1, 0, 2)).reshape(share, model)
    hidden = gelu_exact(preact).astype(BF16)
    slope = gelu_slope(preact)
    hidden = jnp.broadcast_to(hidden.reshape(2, 1, few, model), (2, spread, few, model))
    hidden = hidden.reshape(2 * spread, few, model)
    hidden = lax.all_to_all(hidden, ("row", "col", "vis"), 0, 0, axis_index_groups=column_groups)
    right_o, left_o, far_gate_o, far_up_o = [from_core(w) for w in (right, left, far_gate, far_up)]
    pieces = [weights, right, left, far_gate, far_up, weights_o, right_o, left_o, far_gate_o, far_up_o]
    hidden = hidden.reshape(2, lane, model)

    offset = (x + n_x - vis) % n_x
    part = sum(jnp.where(offset == shifts[k], k, 0) for k in range(n_x))
    part = (part + n_x - quarter) % n_x
    cot = lax.dynamic_slice(cotangent.T, (part * unit, core * lane), (unit, lane))
    cot_pairs = []
    for low in range(n_low):
        for i in range(n_x):
            for v in range(n_vis):
                for q in range(n_quarter):
                    for k in range(2):
                        there = (low * n_x + (i + shifts[(v + q) % n_x]) % n_x) * n_col + 2 * q + k
                        here = (low * n_x + i) * n_col + 2 * q + k
                        cot_pairs.append((there * n_vis + i, here * n_vis + v))
    cot = lax.ppermute(cot, ("row", "col", "vis"), cot_pairs)
    cot = jnp.pad(cot.astype(F32), ((0, pad), (0, 0)))

    rows = 2 * (unit + pad)
    flops = 4 * lane * n_x * rows * model
    place = jnp.stack([core, vis])
    both = with_weights(gate_body, place, hidden, pieces, (n_x, rows, lane), flops)
    sums = lax.all_to_all(both, "col", 0, 0, axis_index_groups=quarter_groups)
    sums = jnp.sum(sums.astype(F32), axis=0)
    gate_sum, up_sum = sums[: unit + pad], sums[unit + pad :]
    sig = jax.nn.sigmoid(gate_sum)
    d_gate = (cot * up_sum * sig * (1.0 + gate_sum * (1.0 - sig))).astype(BF16)
    d_up = (cot * gate_sum * sig).astype(BF16)
    d_both = jnp.concatenate([d_gate, d_up], axis=0)
    d_all = lax.all_gather(d_both, "col", axis=0, axis_index_groups=quarter_groups)

    dact = with_weights(dact_body, place, d_all, pieces, (2, lane, model), flops)
    dact = lax.all_to_all(
        dact.reshape(2 * spread, few, model), ("row", "col", "vis"), 0, 0, axis_index_groups=column_groups
    )
    dact = jnp.sum(dact.reshape(2, spread, few, model).astype(F32), axis=1).reshape(share, model)
    dpre = (dact * slope).astype(BF16)
    dpre = jnp.transpose(dpre.reshape(share, n_vis, width), (1, 0, 2))
    dpre = jnp.broadcast_to(dpre[None], (n_row, n_vis, share, width))
    dpre = lax.all_to_all(
        dpre.reshape(n_x * spread, share, width), ("row", "vis"), 0, 0, axis_index_groups=sheet_groups
    )
    dpre = jnp.transpose(dpre.reshape(n_x, spread, 2, few, width), (0, 2, 1, 3, 4))
    dpre = dpre.reshape(n_tok, width)
    return dot(tokens_t, dpre, ((1,), (0,))).astype(BF16)


def solution(mesh):
    in_specs = (
        P("vis", "row"),
        P(),
        P("row", ("col", "vis")),
        P("col", ("row", "vis")),
        P("col", ("row", "vis")),
        P("vis", "row"),
    )
    out_specs = P("row", ("col", "vis"))
    return jax.shard_map(shards, mesh=mesh, in_specs=in_specs, out_specs=out_specs, check_vma=False)
```

```python
import jax
import jax.numpy as jnp
from jax import lax
from jax.experimental import pallas as pl
from jax.experimental.pallas import tpu as pltpu
from jax.sharding import PartitionSpec as P

TILE = 256
F32 = jnp.float32
BF16 = jnp.bfloat16
KERNEL_VMEM = 60 * 2**20
SMALL_VMEM = 24 * 2**20


def gelu_exact(value):
    return 0.5 * value * (1.0 + lax.erf(value * 0.7071067811865476))


def gelu_slope(value):
    normal_cdf = 0.5 * (1.0 + lax.erf(value * 0.7071067811865476))
    return normal_cdf + value * jnp.exp(-0.5 * value * value) * 0.3989422804014327


def dot(a, b, contract):
    return lax.dot_general(a, b, (contract, ((), ())), preferred_element_type=F32)


def in_vmem(body, n_scalars, out_shape, operands, flops, scratch=()):
    spaces = [pltpu.SMEM] * n_scalars + [pltpu.VMEM] * (len(operands) - n_scalars)
    moved = 2 * sum(a.size for a in operands[n_scalars:])
    return pl.pallas_call(
        body,
        in_specs=[pl.BlockSpec(memory_space=space) for space in spaces],
        out_specs=pl.BlockSpec(memory_space=pltpu.VMEM),
        out_shape=jax.ShapeDtypeStruct(out_shape, BF16),
        scratch_shapes=list(scratch),
        compiler_params=pltpu.CompilerParams(vmem_limit_bytes=SMALL_VMEM),
        cost_estimate=pl.CostEstimate(flops=flops, bytes_accessed=moved, transcendentals=0),
    )(*operands)


def pick_kernel(slot_ref, arrived_ref, out_ref):
    per_group = arrived_ref.shape[2] // TILE
    for t in range(slot_ref.shape[0]):
        slot = slot_ref[t]
        lanes = pl.multiple_of(lax.rem(slot, per_group) * TILE, TILE)
        out_ref[:, t * TILE : (t + 1) * TILE] = arrived_ref[lax.div(slot, per_group), :, pl.ds(lanes, TILE)]


def proj_kernel(place_ref, mine_ref, other_ref, weight_ref, right_hbm, left_hbm, out_ref, low_ref, high_ref, sems):
    first = low_ref.shape[0]
    low_copy = pltpu.make_async_copy(right_hbm.at[pl.ds(0, first)], low_ref, sems.at[0])
    high_copy = pltpu.make_async_copy(left_hbm.at[pl.ds(first, high_ref.shape[0])], high_ref, sems.at[1])
    low_copy.start()
    high_copy.start()
    half = mine_ref.shape[0]
    core = place_ref[0]
    w_mine = weight_ref[pl.ds(pl.multiple_of(core * half, 16), half), :]
    w_other = weight_ref[pl.ds(pl.multiple_of((1 - core) * half, 16), half), :]
    tiles = mine_ref.shape[1] // TILE
    lows, few = out_ref.shape[0] // tiles, out_ref.shape[1] // 2
    for t in range(tiles):
        tokens = slice(t * TILE, (t + 1) * TILE)
        total = dot(mine_ref[:, tokens], w_mine, ((0,), (0,)))
        total = (total + dot(other_ref[:, tokens], w_other, ((0,), (0,)))).astype(BF16)
        for k in range(2):
            for low in range(lows):
                at = (k * lows + low) * few
                out_ref[t * lows + low, k * few : (k + 1) * few, :] = total[at : at + few]
    low_copy.wait()
    high_copy.wait()


def project(place, mine, other, weight, right, left, out_shape, flops):
    rows, model = right.shape
    first = -(rows // -32) * 16
    hbm, vmem = pl.BlockSpec(memory_space=pltpu.HBM), pl.BlockSpec(memory_space=pltpu.VMEM)
    moved = 2 * (mine.size + other.size + weight.size + right.size)
    return pl.pallas_call(
        proj_kernel,
        in_specs=[pl.BlockSpec(memory_space=pltpu.SMEM), vmem, vmem, vmem, hbm, hbm],
        out_specs=(vmem,) * 3,
        out_shape=(
            jax.ShapeDtypeStruct(out_shape, BF16),
            jax.ShapeDtypeStruct((first, model), BF16),
            jax.ShapeDtypeStruct((rows - first, model), BF16),
        ),
        scratch_shapes=[pltpu.SemaphoreType.DMA((2,))],
        compiler_params=pltpu.CompilerParams(vmem_limit_bytes=SMALL_VMEM),
        cost_estimate=pl.CostEstimate(flops=flops, bytes_accessed=moved, transcendentals=0),
    )(place, mine, other, weight, right, left)


def final_kernel(place_ref, mine_ref, other_ref, dpre_ref, out_ref, ordered_ref):
    half = mine_ref.shape[0]
    core = place_ref[0]
    tiles = mine_ref.shape[1] // TILE
    lows, few = dpre_ref.shape[0] // tiles, dpre_ref.shape[1] // 2
    for t in range(tiles):
        for k in range(2):
            for low in range(lows):
                at = t * TILE + (k * lows + low) * few
                ordered_ref[at : at + few, :] = dpre_ref[t * lows + low, k * few : (k + 1) * few, :]
    dpre = ordered_ref[...]
    first = pl.ds(pl.multiple_of(core * half, 16), half)
    second = pl.ds(pl.multiple_of((1 - core) * half, 16), half)
    out_ref[first, :] = dot(mine_ref[...], dpre, ((1,), (0,))).astype(BF16)
    out_ref[second, :] = dot(other_ref[...], dpre, ((1,), (0,))).astype(BF16)


def gate_body(place_ref, h_ref, weights, out_ref, held, sems, turned):
    n = len(weights) // 2
    copies = weight_copies(weights, held, sems)
    for i in range(n):
        copies[i].start()
        copies[i + n].start()
    core, blocks, rows = place_ref[0], out_ref.shape[0], out_ref.shape[1]
    _, lows, n_vis, few, width = h_ref.shape
    for j in range(2):
        slot = core if j == 0 else 1 - core
        for v in range(n_vis):
            block = h_ref[slot, :, v].reshape(lows * few, width)
            at = (j * n_vis + v) * width
            turned[at : at + width, :] = block.astype(F32).T.astype(BF16)
    model = n_vis * width
    block, at = 0, 0
    for i in range(n):
        size = held[i].shape[0]
        copies[i].wait()
        copies[i + n].wait()
        total = dot(held[i][...], turned[:model, :], ((1,), (0,)))
        total = total + dot(held[i + n][...], turned[model:, :], ((1,), (0,)))
        chunk = lax.rem(block + blocks - place_ref[1], blocks)
        out_ref[chunk, at : at + size, :] = total.astype(BF16)
        at += size
        block, at = block + at // rows, at % rows


def dact_body(place_ref, d_ref, weights, out_ref, held, sems, turned):
    n = len(weights) // 2
    copies = weight_copies(weights, held, sems)
    for copy in copies:
        copy.start()
    core, blocks, rows = place_ref[0], d_ref.shape[0], d_ref.shape[1]
    _, lows, n_vis, few, width = out_ref.shape
    for j in range(2):
        for i in range(n):
            copies[j * n + i].wait()
        slot = core if j == 0 else 1 - core
        for v in range(n_vis):
            total, block, at = None, 0, 0
            for i in range(n):
                w = held[j * n + i]
                size = w.shape[0]
                chunk = lax.rem(block + blocks - place_ref[1], blocks)
                term = dot(d_ref[chunk, at : at + size, :], w[:, v * width : (v + 1) * width], ((0,), (0,)))
                total = term if total is None else total + term
                at += size
                block, at = block + at // rows, at % rows
            out_ref[slot, :, v] = total.astype(BF16).reshape(lows, few, width)


def weight_copies(weights, held, sems):
    return [pltpu.make_async_copy(w, b, sems.at[i]) for i, (w, b) in enumerate(zip(weights, held))]


def with_weights(body, place, operand, weights, out_shape, flops, turned):
    n = len(weights)

    def kernel(place_ref, operand_ref, *refs):
        body(place_ref, operand_ref, refs[:n], refs[n], refs[n + 1 : -2], refs[-2], refs[-1])

    moved = sum(w.size for w in weights) + operand.size
    return pl.pallas_call(
        kernel,
        in_specs=[pl.BlockSpec(memory_space=pltpu.SMEM), pl.BlockSpec(memory_space=pltpu.VMEM)]
        + [pl.BlockSpec(memory_space=pltpu.HBM)] * n,
        out_specs=pl.BlockSpec(memory_space=pltpu.VMEM),
        out_shape=jax.ShapeDtypeStruct(out_shape, BF16),
        scratch_shapes=[pltpu.VMEM(w.shape, BF16) for w in weights]
        + [pltpu.SemaphoreType.DMA((n,)), pltpu.VMEM(turned, BF16)],
        compiler_params=pltpu.CompilerParams(vmem_limit_bytes=KERNEL_VMEM),
        cost_estimate=pl.CostEstimate(flops=flops, bytes_accessed=2 * moved, transcendentals=0),
    )(place, operand, *weights)


def shards(tile_rows, tile_slot, proj_weight, gate_weight, up_weight, cotangent):
    n_vis, n_row, n_col = lax.axis_size("vis"), lax.axis_size("row"), lax.axis_size("col")
    n_x = tile_slot.shape[0]
    n_low = n_row // n_x
    n_quarter = n_col // 2
    row, col, vis = lax.axis_index("row"), lax.axis_index("col"), lax.axis_index("vis")
    core, quarter, x = col % 2, col // 2, row % n_x
    place = jnp.stack([core, vis])
    features = tile_rows.shape[1]
    half = features // 2
    core_pairs = [(2 * i + k, 2 * i + 1 - k) for i in range(n_quarter) for k in range(2)]
    quarter_groups = [[2 * i + k for i in range(n_quarter)] for k in range(2)]
    row_groups = [[low * n_x + i for i in range(n_x) for low in range(n_low)]]
    column_groups = [
        [
            ((low * n_x + i) * n_col + 2 * q + k) * n_vis + v
            for k in range(2)
            for low in range(n_low)
            for v in range(n_vis)
        ]
        for i in range(n_x)
        for q in range(n_quarter)
    ]
    shifts = [0, 1, 3, 2]

    def from_x(value, shift):
        pairs = [
            (low * n_x + i, low * n_x + (i - shift) % n_x) for low in range(n_low) for i in range(n_x)
        ]
        return lax.ppermute(value, "row", pairs)

    def from_core(value):
        return lax.ppermute(value, "col", core_pairs)

    own_half = lax.dynamic_slice_in_dim(tile_rows.T, core * half, half, 0)
    own_half = jnp.broadcast_to(own_half[None], (n_vis,) + own_half.shape)
    arrived = lax.all_to_all(own_half, "vis", 0, 0)
    unit = gate_weight.shape[1]
    pad = -unit % 8
    weights = jnp.stack([gate_weight.T, up_weight.T])
    weights = jnp.pad(weights, ((0, 0), (0, pad), (0, 0))).reshape(2 * (unit + pad), -1)
    right, left, weights_o = from_x(weights, 1), from_x(weights, -1), from_core(weights)
    mine = in_vmem(pick_kernel, 1, (half, n_x * TILE), (tile_slot, arrived), 0)
    other = from_core(mine)
    other, right, left, weights_o = lax.optimization_barrier((other, right, left, weights_o))

    n_tok, width = n_x * TILE, proj_weight.shape[1]
    share, lane, model = n_tok // n_row, TILE // 2, n_vis * width
    few = share // 2
    flops = 2 * n_tok * features * width
    partial, far_low, far_high = project(
        place, mine, other, proj_weight, right, left, (n_row, share, width), flops
    )
    partial = lax.all_to_all(partial, "row", 0, 0, axis_index_groups=row_groups)
    far_low, far_high = from_x(far_low, 1), from_x(far_high, -1)
    preact = jnp.sum(partial.astype(F32), axis=0)
    hidden = gelu_exact(preact).astype(BF16)
    slope = gelu_slope(preact)

    spread = n_low * n_vis
    hidden = jnp.broadcast_to(hidden.reshape(2, 1, few, width), (2, spread, few, width))
    hidden, far_low, far_high = lax.optimization_barrier((hidden, far_low, far_high))
    hidden = lax.all_to_all(
        hidden.reshape(2 * spread, few, width), ("row", "col", "vis"), 0, 0, axis_index_groups=column_groups
    )
    hidden = hidden.reshape(2, n_low, n_vis, few, width)
    pieces = [weights, right, left, far_low, far_high]
    pieces += [weights_o] + [from_core(w) for w in pieces[1:]]

    offset = (x + n_x - vis) % n_x
    part = sum(jnp.where(offset == shifts[k], k, 0) for k in range(n_x))
    part = (part + n_x - quarter) % n_x
    cot = lax.dynamic_slice(cotangent.T, (part * unit, core * lane), (unit, lane))
    cot_pairs = []
    for low in range(n_low):
        for i in range(n_x):
            for v in range(n_vis):
                for q in range(n_quarter):
                    for k in range(2):
                        there = (low * n_x + (i + shifts[(v + q) % n_x]) % n_x) * n_col + 2 * q + k
                        here = (low * n_x + i) * n_col + 2 * q + k
                        cot_pairs.append((there * n_vis + i, here * n_vis + v))
    cot = lax.ppermute(cot, ("row", "col", "vis"), cot_pairs)
    cot = jnp.pad(cot.astype(F32), ((0, pad), (0, 0)))

    rows = 2 * (unit + pad)
    flops = 4 * lane * n_x * rows * model
    both = with_weights(gate_body, place, hidden, pieces, (n_x, rows, lane), flops, (2 * model, lane))
    sums = lax.all_to_all(both, "col", 0, 0, axis_index_groups=quarter_groups)
    sums = jnp.sum(sums.astype(F32), axis=0)
    gate_sum, up_sum = sums[: unit + pad], sums[unit + pad :]
    sig = jax.nn.sigmoid(gate_sum)
    d_gate = (cot * up_sum * sig * (1.0 + gate_sum * (1.0 - sig))).astype(BF16)
    d_up = (cot * gate_sum * sig).astype(BF16)
    d_both = jnp.concatenate([d_gate, d_up], axis=0)
    d_all = lax.all_gather(d_both, "col", axis=0, axis_index_groups=quarter_groups)

    shape = (2, n_low, n_vis, few, width)
    dact = with_weights(dact_body, place, d_all, pieces, shape, flops, (16, lane))
    dact = lax.all_to_all(
        dact.reshape(2 * spread, few, width), ("row", "col", "vis"), 0, 0, axis_index_groups=column_groups
    )
    dact = jnp.sum(dact.reshape(2, spread, few, width).astype(F32), axis=1).reshape(share, width)
    dpre = (dact * slope).astype(BF16)
    dpre = lax.all_to_all(
        jnp.broadcast_to(dpre[None], (n_row, share, width)), "row", 0, 0, axis_index_groups=row_groups
    )
    flops = 2 * n_tok * features * width
    return in_vmem(
        final_kernel, 1, (features, width), (place, mine, other, dpre), flops,
        scratch=[pltpu.VMEM((n_tok, width), BF16)],
    )


def solution(mesh):
    in_specs = (
        P("vis", "row"),
        P(),
        P("row", ("col", "vis")),
        P("col", ("row", "vis")),
        P("col", ("row", "vis")),
        P("vis", "row"),
    )
    out_specs = P("row", ("col", "vis"))
    return jax.shard_map(shards, mesh=mesh, in_specs=in_specs, out_specs=out_specs, check_vma=False)
```

```python
import jax
import jax.numpy as jnp
from jax import lax
from jax.experimental import pallas as pl
from jax.experimental.pallas import tpu as pltpu
from jax.sharding import PartitionSpec as P

TILE = 256
F32 = jnp.float32
BF16 = jnp.bfloat16
KERNEL_VMEM = 60 * 2**20
SMALL_VMEM = 24 * 2**20


def gelu_exact(value):
    return 0.5 * value * (1.0 + lax.erf(value * 0.7071067811865476))


def gelu_slope(value):
    normal_cdf = 0.5 * (1.0 + lax.erf(value * 0.7071067811865476))
    return normal_cdf + value * jnp.exp(-0.5 * value * value) * 0.3989422804014327


def dot(a, b, contract):
    return lax.dot_general(a, b, (contract, ((), ())), preferred_element_type=F32)


def in_vmem(body, n_scalars, out_shape, operands, flops, scratch=()):
    spaces = [pltpu.SMEM] * n_scalars + [pltpu.VMEM] * (len(operands) - n_scalars)
    moved = 2 * sum(a.size for a in operands[n_scalars:])
    return pl.pallas_call(
        body,
        in_specs=[pl.BlockSpec(memory_space=space) for space in spaces],
        out_specs=pl.BlockSpec(memory_space=pltpu.VMEM),
        out_shape=jax.ShapeDtypeStruct(out_shape, BF16),
        scratch_shapes=list(scratch),
        compiler_params=pltpu.CompilerParams(vmem_limit_bytes=SMALL_VMEM),
        cost_estimate=pl.CostEstimate(flops=flops, bytes_accessed=moved, transcendentals=0),
    )(*operands)


def pick_kernel(slot_ref, arrived_ref, out_ref):
    per_group = arrived_ref.shape[2] // TILE
    for t in range(slot_ref.shape[0]):
        slot = slot_ref[t]
        lanes = pl.multiple_of(lax.rem(slot, per_group) * TILE, TILE)
        out_ref[:, t * TILE : (t + 1) * TILE] = arrived_ref[lax.div(slot, per_group), :, pl.ds(lanes, TILE)]


def proj_kernel(place_ref, mine_ref, other_ref, weight_ref, out_ref):
    half = mine_ref.shape[0]
    core = place_ref[0]
    w_mine = weight_ref[pl.ds(pl.multiple_of(core * half, 16), half), :]
    w_other = weight_ref[pl.ds(pl.multiple_of((1 - core) * half, 16), half), :]
    tiles = mine_ref.shape[1] // TILE
    lows, few = out_ref.shape[0] // tiles, out_ref.shape[1] // 2
    for t in range(tiles):
        tokens = slice(t * TILE, (t + 1) * TILE)
        total = dot(mine_ref[:, tokens], w_mine, ((0,), (0,)))
        total = (total + dot(other_ref[:, tokens], w_other, ((0,), (0,)))).astype(BF16)
        for k in range(2):
            for low in range(lows):
                at = (k * lows + low) * few
                out_ref[t * lows + low, k * few : (k + 1) * few, :] = total[at : at + few]


def final_kernel(place_ref, mine_ref, other_ref, dpre_ref, out_ref, ordered_ref):
    half = mine_ref.shape[0]
    core = place_ref[0]
    tiles = mine_ref.shape[1] // TILE
    lows, few = dpre_ref.shape[0] // tiles, dpre_ref.shape[1] // 2
    for t in range(tiles):
        for k in range(2):
            for low in range(lows):
                at = t * TILE + (k * lows + low) * few
                ordered_ref[at : at + few, :] = dpre_ref[t * lows + low, k * few : (k + 1) * few, :]
    dpre = ordered_ref[...]
    first = pl.ds(pl.multiple_of(core * half, 16), half)
    second = pl.ds(pl.multiple_of((1 - core) * half, 16), half)
    out_ref[first, :] = dot(mine_ref[...], dpre, ((1,), (0,))).astype(BF16)
    out_ref[second, :] = dot(other_ref[...], dpre, ((1,), (0,))).astype(BF16)


def gate_body(place_ref, h_ref, weights, out_ref, held, sems, turned):
    n = len(weights) // 2
    copies = weight_copies(weights, held, sems)
    for i in range(n):
        copies[i].start()
        copies[i + n].start()
    core, blocks, rows = place_ref[0], out_ref.shape[0], out_ref.shape[1]
    _, lows, n_vis, few, width = h_ref.shape
    for j in range(2):
        slot = core if j == 0 else 1 - core
        for v in range(n_vis):
            block = h_ref[slot, :, v].reshape(lows * few, width)
            at = (j * n_vis + v) * width
            turned[at : at + width, :] = block.astype(F32).T.astype(BF16)
    model = n_vis * width
    block, at = 0, 0
    for i in range(n):
        size = held[i].shape[0]
        copies[i].wait()
        copies[i + n].wait()
        total = dot(held[i][...], turned[:model, :], ((1,), (0,)))
        total = total + dot(held[i + n][...], turned[model:, :], ((1,), (0,)))
        chunk = lax.rem(block + blocks - place_ref[1], blocks)
        out_ref[chunk, at : at + size, :] = total.astype(BF16)
        at += size
        block, at = block + at // rows, at % rows


def dact_body(place_ref, d_ref, weights, out_ref, held, sems, turned):
    n = len(weights) // 2
    copies = weight_copies(weights, held, sems)
    for copy in copies:
        copy.start()
    core, blocks, rows = place_ref[0], d_ref.shape[0], d_ref.shape[1]
    _, lows, n_vis, few, width = out_ref.shape
    for j in range(2):
        for i in range(n):
            copies[j * n + i].wait()
        slot = core if j == 0 else 1 - core
        for v in range(n_vis):
            total, block, at = None, 0, 0
            for i in range(n):
                w = held[j * n + i]
                size = w.shape[0]
                chunk = lax.rem(block + blocks - place_ref[1], blocks)
                term = dot(d_ref[chunk, at : at + size, :], w[:, v * width : (v + 1) * width], ((0,), (0,)))
                total = term if total is None else total + term
                at += size
                block, at = block + at // rows, at % rows
            out_ref[slot, :, v] = total.astype(BF16).reshape(lows, few, width)


def weight_copies(weights, held, sems):
    return [pltpu.make_async_copy(w, b, sems.at[i]) for i, (w, b) in enumerate(zip(weights, held))]


def with_weights(body, place, operand, weights, out_shape, flops, turned, limit):
    n = len(weights)

    def kernel(place_ref, operand_ref, *refs):
        body(place_ref, operand_ref, refs[:n], refs[n], refs[n + 1 : -2], refs[-2], refs[-1])

    moved = sum(w.size for w in weights) + operand.size
    return pl.pallas_call(
        kernel,
        in_specs=[pl.BlockSpec(memory_space=pltpu.SMEM), pl.BlockSpec(memory_space=pltpu.VMEM)]
        + [pl.BlockSpec(memory_space=pltpu.HBM)] * n,
        out_specs=pl.BlockSpec(memory_space=pltpu.VMEM),
        out_shape=jax.ShapeDtypeStruct(out_shape, BF16),
        scratch_shapes=[pltpu.VMEM(w.shape, BF16) for w in weights]
        + [pltpu.SemaphoreType.DMA((n,)), pltpu.VMEM(turned, BF16)],
        compiler_params=pltpu.CompilerParams(vmem_limit_bytes=limit),
        cost_estimate=pl.CostEstimate(flops=flops, bytes_accessed=2 * moved, transcendentals=0),
    )(place, operand, *weights)


def shards(tile_rows, tile_slot, proj_weight, gate_weight, up_weight, cotangent):
    n_vis, n_row, n_col = lax.axis_size("vis"), lax.axis_size("row"), lax.axis_size("col")
    n_x = tile_slot.shape[0]
    n_low = n_row // n_x
    n_quarter = n_col // 2
    row, col, vis = lax.axis_index("row"), lax.axis_index("col"), lax.axis_index("vis")
    core, quarter, x = col % 2, col // 2, row % n_x
    place = jnp.stack([core, vis])
    features = tile_rows.shape[1]
    half = features // 2
    core_pairs = [(2 * i + k, 2 * i + 1 - k) for i in range(n_quarter) for k in range(2)]
    quarter_groups = [[2 * i + k for i in range(n_quarter)] for k in range(2)]
    row_groups = [[low * n_x + i for i in range(n_x) for low in range(n_low)]]
    column_groups = [
        [
            ((low * n_x + i) * n_col + 2 * q + k) * n_vis + v
            for k in range(2)
            for low in range(n_low)
            for v in range(n_vis)
        ]
        for i in range(n_x)
        for q in range(n_quarter)
    ]
    shifts = [0, 1, 3, 2]

    def from_x(value, shift):
        pairs = [
            (low * n_x + i, low * n_x + (i - shift) % n_x) for low in range(n_low) for i in range(n_x)
        ]
        return lax.ppermute(value, "row", pairs)

    def from_core(value):
        return lax.ppermute(value, "col", core_pairs)

    own_half = lax.dynamic_slice_in_dim(tile_rows.T, core * half, half, 0)
    own_half = jnp.broadcast_to(own_half[None], (n_vis,) + own_half.shape)
    arrived = lax.all_to_all(own_half, "vis", 0, 0)
    unit = gate_weight.shape[1]
    pad = -unit % 8
    weights = jnp.stack([gate_weight.T, up_weight.T])
    weights = jnp.pad(weights, ((0, 0), (0, pad), (0, 0))).reshape(2 * (unit + pad), -1)
    right, left, weights_o = from_x(weights, 1), from_x(weights, -1), from_core(weights)
    mine = in_vmem(pick_kernel, 1, (half, n_x * TILE), (tile_slot, arrived), 0)
    other = from_core(mine)

    n_tok, width = n_x * TILE, proj_weight.shape[1]
    share, lane, model = n_tok // n_row, TILE // 2, n_vis * width
    few = share // 2
    flops = 2 * n_tok * features * width
    partial = in_vmem(proj_kernel, 1, (n_row, share, width), (place, mine, other, proj_weight), flops)
    partial, right, left, weights_o = lax.optimization_barrier((partial, right, left, weights_o))
    first = -((unit + pad) // -16) * 16
    far_low, far_high = right[:first], left[first:]
    partial = lax.all_to_all(partial, "row", 0, 0, axis_index_groups=row_groups)
    far_low, far_high = from_x(far_low, 1), from_x(far_high, -1)
    preact = jnp.sum(partial.astype(F32), axis=0)
    hidden = gelu_exact(preact).astype(BF16)
    slope = gelu_slope(preact)

    spread = n_low * n_vis
    hidden = jnp.broadcast_to(hidden.reshape(2, 1, few, width), (2, spread, few, width))
    hidden, far_low, far_high = lax.optimization_barrier((hidden, far_low, far_high))
    hidden = lax.all_to_all(
        hidden.reshape(2 * spread, few, width), ("row", "col", "vis"), 0, 0, axis_index_groups=column_groups
    )
    hidden = hidden.reshape(2, n_low, n_vis, few, width)
    pieces = [weights, right, left, far_low, far_high]
    pieces += [weights_o] + [from_core(w) for w in pieces[1:]]

    offset = (x + n_x - vis) % n_x
    part = sum(jnp.where(offset == shifts[k], k, 0) for k in range(n_x))
    part = (part + n_x - quarter) % n_x
    cot = lax.dynamic_slice(cotangent.T, (part * unit, core * lane), (unit, lane))
    cot_pairs = []
    for low in range(n_low):
        for i in range(n_x):
            for v in range(n_vis):
                for q in range(n_quarter):
                    for k in range(2):
                        there = (low * n_x + (i + shifts[(v + q) % n_x]) % n_x) * n_col + 2 * q + k
                        here = (low * n_x + i) * n_col + 2 * q + k
                        cot_pairs.append((there * n_vis + i, here * n_vis + v))
    cot = lax.ppermute(cot, ("row", "col", "vis"), cot_pairs)
    cot = jnp.pad(cot.astype(F32), ((0, pad), (0, 0)))

    rows = 2 * (unit + pad)
    flops = 4 * lane * n_x * rows * model
    both = with_weights(gate_body, place, hidden, pieces, (n_x, rows, lane), flops, (2 * model, lane), KERNEL_VMEM)
    sums = lax.all_to_all(both, "col", 0, 0, axis_index_groups=quarter_groups)
    sums = jnp.sum(sums.astype(F32), axis=0)
    gate_sum, up_sum = sums[: unit + pad], sums[unit + pad :]
    sig = jax.nn.sigmoid(gate_sum)
    d_gate = (cot * up_sum * sig * (1.0 + gate_sum * (1.0 - sig))).astype(BF16)
    d_up = (cot * gate_sum * sig).astype(BF16)
    d_both = jnp.concatenate([d_gate, d_up], axis=0)
    d_all = lax.all_gather(d_both, "col", axis=0, axis_index_groups=quarter_groups)

    shape = (2, n_low, n_vis, few, width)
    dact = with_weights(dact_body, place, d_all, pieces, shape, flops, (16, lane), SMALL_VMEM)
    dact = lax.all_to_all(
        dact.reshape(2 * spread, few, width), ("row", "col", "vis"), 0, 0, axis_index_groups=column_groups
    )
    dact = jnp.sum(dact.reshape(2, spread, few, width).astype(F32), axis=1).reshape(share, width)
    dpre = (dact * slope).astype(BF16)
    dpre = lax.all_to_all(
        jnp.broadcast_to(dpre[None], (n_row, share, width)), "row", 0, 0, axis_index_groups=row_groups
    )
    flops = 2 * n_tok * features * width
    return in_vmem(
        final_kernel, 1, (features, width), (place, mine, other, dpre), flops,
        scratch=[pltpu.VMEM((n_tok, width), BF16)],
    )


def solution(mesh):
    in_specs = (
        P("vis", "row"),
        P(),
        P("row", ("col", "vis")),
        P("col", ("row", "vis")),
        P("col", ("row", "vis")),
        P("vis", "row"),
    )
    out_specs = P("row", ("col", "vis"))
    return jax.shard_map(shards, mesh=mesh, in_specs=in_specs, out_specs=out_specs, check_vma=False)
```

```python
import jax
import jax.numpy as jnp
from jax import lax
from jax.experimental import pallas as pl
from jax.experimental.pallas import tpu as pltpu
from jax.sharding import PartitionSpec as P

TILE = 256
F32 = jnp.float32
BF16 = jnp.bfloat16
KERNEL_VMEM = 60 * 2**20
SMALL_VMEM = 48 * 2**20
PICK_VMEM = 52 * 2**20


def gelu_exact(value):
    return 0.5 * value * (1.0 + lax.erf(value * 0.7071067811865476))


def gelu_slope(value):
    normal_cdf = 0.5 * (1.0 + lax.erf(value * 0.7071067811865476))
    return normal_cdf + value * jnp.exp(-0.5 * value * value) * 0.3989422804014327


def dot(a, b, contract):
    return lax.dot_general(a, b, (contract, ((), ())), preferred_element_type=F32)


def in_vmem(body, n_scalars, out_shape, operands, flops, scratch=(), limit=SMALL_VMEM):
    spaces = [pltpu.SMEM] * n_scalars + [pltpu.VMEM] * (len(operands) - n_scalars)
    moved = 2 * sum(a.size for a in operands[n_scalars:])
    return pl.pallas_call(
        body,
        in_specs=[pl.BlockSpec(memory_space=space) for space in spaces],
        out_specs=pl.BlockSpec(memory_space=pltpu.VMEM),
        out_shape=jax.ShapeDtypeStruct(out_shape, BF16),
        scratch_shapes=list(scratch),
        compiler_params=pltpu.CompilerParams(vmem_limit_bytes=limit),
        cost_estimate=pl.CostEstimate(flops=flops, bytes_accessed=moved, transcendentals=0),
    )(*operands)


def pick_kernel(slot_ref, arrived_ref, out_ref):
    per_group = arrived_ref.shape[2] // TILE
    for t in range(slot_ref.shape[0]):
        slot = slot_ref[t]
        lanes = pl.multiple_of(lax.rem(slot, per_group) * TILE, TILE)
        out_ref[:, t * TILE : (t + 1) * TILE] = arrived_ref[lax.div(slot, per_group), :, pl.ds(lanes, TILE)]


def proj_kernel(place_ref, mine_ref, other_ref, weight_ref, out_ref):
    half = mine_ref.shape[0]
    core = place_ref[0]
    w_mine = weight_ref[pl.ds(pl.multiple_of(core * half, 16), half), :]
    w_other = weight_ref[pl.ds(pl.multiple_of((1 - core) * half, 16), half), :]
    tiles = mine_ref.shape[1] // TILE
    lows, few = out_ref.shape[0] // tiles, out_ref.shape[1] // 2
    for t in range(tiles):
        tokens = slice(t * TILE, (t + 1) * TILE)
        total = dot(mine_ref[:, tokens], w_mine, ((0,), (0,)))
        total = (total + dot(other_ref[:, tokens], w_other, ((0,), (0,)))).astype(BF16)
        for k in range(2):
            for low in range(lows):
                at = (k * lows + low) * few
                out_ref[t * lows + low, k * few : (k + 1) * few, :] = total[at : at + few]


def final_kernel(place_ref, mine_ref, other_ref, dpre_ref, out_ref, ordered_ref):
    half = mine_ref.shape[0]
    core = place_ref[0]
    tiles = mine_ref.shape[1] // TILE
    lows, few = dpre_ref.shape[0] // tiles, dpre_ref.shape[1] // 2
    for t in range(tiles):
        for k in range(2):
            for low in range(lows):
                at = t * TILE + (k * lows + low) * few
                ordered_ref[at : at + few, :] = dpre_ref[t * lows + low, k * few : (k + 1) * few, :]
    dpre = ordered_ref[...]
    first = pl.ds(pl.multiple_of(core * half, 16), half)
    second = pl.ds(pl.multiple_of((1 - core) * half, 16), half)
    out_ref[first, :] = dot(mine_ref[...], dpre, ((1,), (0,))).astype(BF16)
    out_ref[second, :] = dot(other_ref[...], dpre, ((1,), (0,))).astype(BF16)


def gate_kernel(place_ref, h_hbm, *refs):
    n = (len(refs) - 5) // 4
    weights, out_hbm, held = refs[: 2 * n], refs[2 * n], refs[2 * n + 1 : 4 * n + 1]
    h, turned, out, sems = refs[4 * n + 1 :]
    loads = weight_copies(weights, held, sems)
    load_h = pltpu.make_async_copy(h_hbm, h, sems.at[2 * n])
    load_h.start()
    for i in range(n):
        loads[i].start()
        loads[i + n].start()
    core, blocks, rows = place_ref[0], out.shape[0], out.shape[1]
    _, lows, n_vis, few, width = h.shape
    model = n_vis * width
    load_h.wait()
    for j in range(2):
        slot = core if j == 0 else 1 - core
        for v in range(n_vis):
            block = h[slot, :, v].reshape(lows * few, width)
            at = (j * n_vis + v) * width
            turned[at : at + width, :] = block.astype(F32).T.astype(BF16)
    stores = []
    block, at = 0, 0
    for i in range(n):
        size = held[i].shape[0]
        loads[i].wait()
        loads[i + n].wait()
        total = dot(held[i][...], turned[:model, :], ((1,), (0,)))
        total = total + dot(held[i + n][...], turned[model:, :], ((1,), (0,)))
        out[block, at : at + size, :] = total.astype(BF16)
        at += size
        if at == rows:
            chunk = lax.rem(block + blocks - place_ref[1], blocks)
            stores.append(pltpu.make_async_copy(out.at[block], out_hbm.at[chunk], sems.at[2 * n + 1 + block]))
            stores[-1].start()
            block, at = block + 1, 0
    for store in stores:
        store.wait()


def gate_up(place, hidden, weights, out_shape, flops, turned):
    n = len(weights)
    hbm = pl.BlockSpec(memory_space=pltpu.HBM)
    moved = sum(w.size for w in weights) + hidden.size
    return pl.pallas_call(
        gate_kernel,
        in_specs=[pl.BlockSpec(memory_space=pltpu.SMEM)] + [hbm] * (n + 1),
        out_specs=hbm,
        out_shape=jax.ShapeDtypeStruct(out_shape, BF16),
        scratch_shapes=[pltpu.VMEM(w.shape, BF16) for w in weights]
        + [pltpu.VMEM(hidden.shape, BF16), pltpu.VMEM(turned, BF16), pltpu.VMEM(out_shape, BF16)]
        + [pltpu.SemaphoreType.DMA((n + 1 + out_shape[0],))],
        compiler_params=pltpu.CompilerParams(vmem_limit_bytes=KERNEL_VMEM),
        cost_estimate=pl.CostEstimate(flops=flops, bytes_accessed=2 * moved, transcendentals=0),
    )(place, hidden, *weights)


def dact_body(place_ref, d_ref, weights, out_ref, held, sems, turned):
    n = len(weights) // 2
    copies = weight_copies(weights, held, sems)
    for copy in copies:
        copy.start()
    core, blocks, rows = place_ref[0], d_ref.shape[0], d_ref.shape[1]
    _, lows, n_vis, few, width = out_ref.shape
    for j in range(2):
        for i in range(n):
            copies[j * n + i].wait()
        slot = core if j == 0 else 1 - core
        for v in range(n_vis):
            total, block, at = None, 0, 0
            for i in range(n):
                w = held[j * n + i]
                size = w.shape[0]
                chunk = lax.rem(block + blocks - place_ref[1], blocks)
                term = dot(d_ref[chunk, at : at + size, :], w[:, v * width : (v + 1) * width], ((0,), (0,)))
                total = term if total is None else total + term
                at += size
                block, at = block + at // rows, at % rows
            out_ref[slot, :, v] = total.astype(BF16).reshape(lows, few, width)


def weight_copies(weights, held, sems):
    return [pltpu.make_async_copy(w, b, sems.at[i]) for i, (w, b) in enumerate(zip(weights, held))]


def with_weights(body, place, operand, weights, out_shape, flops, turned, limit):
    n = len(weights)

    def kernel(place_ref, operand_ref, *refs):
        body(place_ref, operand_ref, refs[:n], refs[n], refs[n + 1 : -2], refs[-2], refs[-1])

    moved = sum(w.size for w in weights) + operand.size
    return pl.pallas_call(
        kernel,
        in_specs=[pl.BlockSpec(memory_space=pltpu.SMEM), pl.BlockSpec(memory_space=pltpu.VMEM)]
        + [pl.BlockSpec(memory_space=pltpu.HBM)] * n,
        out_specs=pl.BlockSpec(memory_space=pltpu.VMEM),
        out_shape=jax.ShapeDtypeStruct(out_shape, BF16),
        scratch_shapes=[pltpu.VMEM(w.shape, BF16) for w in weights]
        + [pltpu.SemaphoreType.DMA((n,)), pltpu.VMEM(turned, BF16)],
        compiler_params=pltpu.CompilerParams(vmem_limit_bytes=limit),
        cost_estimate=pl.CostEstimate(flops=flops, bytes_accessed=2 * moved, transcendentals=0),
    )(place, operand, *weights)


def shards(tile_rows, tile_slot, proj_weight, gate_weight, up_weight, cotangent):
    n_vis, n_row, n_col = lax.axis_size("vis"), lax.axis_size("row"), lax.axis_size("col")
    n_x = tile_slot.shape[0]
    n_low = n_row // n_x
    n_quarter = n_col // 2
    row, col, vis = lax.axis_index("row"), lax.axis_index("col"), lax.axis_index("vis")
    core, quarter, x = col % 2, col // 2, row % n_x
    place = jnp.stack([core, vis])
    features = tile_rows.shape[1]
    half = features // 2
    core_pairs = [(2 * i + k, 2 * i + 1 - k) for i in range(n_quarter) for k in range(2)]
    quarter_groups = [[2 * i + k for i in range(n_quarter)] for k in range(2)]
    row_groups = [[low * n_x + i for i in range(n_x) for low in range(n_low)]]
    column_groups = [
        [
            ((low * n_x + i) * n_col + 2 * q + k) * n_vis + v
            for k in range(2)
            for low in range(n_low)
            for v in range(n_vis)
        ]
        for i in range(n_x)
        for q in range(n_quarter)
    ]
    shifts = [0, 1, 3, 2]

    def from_x(value, shift):
        pairs = [
            (low * n_x + i, low * n_x + (i - shift) % n_x) for low in range(n_low) for i in range(n_x)
        ]
        return lax.ppermute(value, "row", pairs)

    def from_core(value):
        return lax.ppermute(value, "col", core_pairs)

    own_half = lax.dynamic_slice_in_dim(tile_rows.T, core * half, half, 0)
    own_half = jnp.broadcast_to(own_half[None], (n_vis,) + own_half.shape)
    arrived = lax.all_to_all(own_half, "vis", 0, 0)
    unit = gate_weight.shape[1]
    pad = -unit % 8
    weights = jnp.stack([gate_weight.T, up_weight.T])
    weights = jnp.pad(weights, ((0, 0), (0, pad), (0, 0))).reshape(2 * (unit + pad), -1)
    right, left, weights_o = from_x(weights, 1), from_x(weights, -1), from_core(weights)
    mine = in_vmem(pick_kernel, 1, (half, n_x * TILE), (tile_slot, arrived), 0, limit=PICK_VMEM)
    other = from_core(mine)

    n_tok, width = n_x * TILE, proj_weight.shape[1]
    share, lane, model = n_tok // n_row, TILE // 2, n_vis * width
    few = share // 2
    flops = 2 * n_tok * features * width
    partial = in_vmem(proj_kernel, 1, (n_row, share, width), (place, mine, other, proj_weight), flops)
    partial, right, left, weights_o = lax.optimization_barrier((partial, right, left, weights_o))
    first = -(weights.shape[0] * 11 // -320) * 16
    far_low, far_high = right[:first], left[first:]
    partial = lax.all_to_all(partial, "row", 0, 0, axis_index_groups=row_groups)
    far_low, far_high = from_x(far_low, 1), from_x(far_high, -1)
    preact = jnp.sum(partial.astype(F32), axis=0)
    hidden = gelu_exact(preact).astype(BF16)
    slope = gelu_slope(preact)

    spread = n_low * n_vis
    hidden = jnp.broadcast_to(hidden.reshape(2, 1, few, width), (2, spread, few, width))
    hidden, far_low, far_high = lax.optimization_barrier((hidden, far_low, far_high))
    hidden = lax.all_to_all(
        hidden.reshape(2 * spread, few, width), ("row", "col", "vis"), 0, 0, axis_index_groups=column_groups
    )
    hidden = hidden.reshape(2, n_low, n_vis, few, width)
    pieces = [weights, right, left, far_low, far_high]
    pieces += [weights_o] + [from_core(w) for w in pieces[1:]]

    offset = (x + n_x - vis) % n_x
    part = sum(jnp.where(offset == shifts[k], k, 0) for k in range(n_x))
    part = (part + n_x - quarter) % n_x
    cot = lax.dynamic_slice(cotangent.T, (part * unit, core * lane), (unit, lane))
    cot_pairs = []
    for low in range(n_low):
        for i in range(n_x):
            for v in range(n_vis):
                for q in range(n_quarter):
                    for k in range(2):
                        there = (low * n_x + (i + shifts[(v + q) % n_x]) % n_x) * n_col + 2 * q + k
                        here = (low * n_x + i) * n_col + 2 * q + k
                        cot_pairs.append((there * n_vis + i, here * n_vis + v))
    cot = lax.ppermute(cot, ("row", "col", "vis"), cot_pairs)
    cot = jnp.pad(cot.astype(F32), ((0, pad), (0, 0)))

    rows = 2 * (unit + pad)
    flops = 4 * lane * n_x * rows * model
    both = gate_up(place, hidden, pieces, (n_x, rows, lane), flops, (2 * model, lane))
    sums = lax.all_to_all(both, "col", 0, 0, axis_index_groups=quarter_groups)
    sums = jnp.sum(sums.astype(F32), axis=0)
    gate_sum, up_sum = sums[: unit + pad], sums[unit + pad :]
    sig = jax.nn.sigmoid(gate_sum)
    d_gate = (cot * up_sum * sig * (1.0 + gate_sum * (1.0 - sig))).astype(BF16)
    d_up = (cot * gate_sum * sig).astype(BF16)
    d_both = jnp.concatenate([d_gate, d_up], axis=0)
    d_all = lax.all_gather(d_both, "col", axis=0, axis_index_groups=quarter_groups)

    shape = (2, n_low, n_vis, few, width)
    dact = with_weights(dact_body, place, d_all, pieces, shape, flops, (16, lane), SMALL_VMEM)
    dact = lax.all_to_all(
        dact.reshape(2 * spread, few, width), ("row", "col", "vis"), 0, 0, axis_index_groups=column_groups
    )
    dact = jnp.sum(dact.reshape(2, spread, few, width).astype(F32), axis=1).reshape(share, width)
    dpre = (dact * slope).astype(BF16)
    dpre = lax.all_to_all(
        jnp.broadcast_to(dpre[None], (n_row, share, width)), "row", 0, 0, axis_index_groups=row_groups
    )
    flops = 2 * n_tok * features * width
    return in_vmem(
        final_kernel, 1, (features, width), (place, mine, other, dpre), flops,
        scratch=[pltpu.VMEM((n_tok, width), BF16)],
    )


def solution(mesh):
    in_specs = (
        P("vis", "row"),
        P(),
        P("row", ("col", "vis")),
        P("col", ("row", "vis")),
        P("col", ("row", "vis")),
        P("vis", "row"),
    )
    out_specs = P("row", ("col", "vis"))
    return jax.shard_map(shards, mesh=mesh, in_specs=in_specs, out_specs=out_specs, check_vma=False)
```

```python
import jax
import jax.numpy as jnp
from jax import lax
from jax.experimental import pallas as pl
from jax.experimental.pallas import tpu as pltpu
from jax.sharding import PartitionSpec as P

TILE = 256
F32 = jnp.float32
BF16 = jnp.bfloat16
KERNEL_VMEM = 60 * 2**20
SMALL_VMEM = 24 * 2**20
DACT_VMEM = 48 * 2**20
PICK_VMEM = 52 * 2**20


def gelu_exact(value):
    return 0.5 * value * (1.0 + lax.erf(value * 0.7071067811865476))


def gelu_slope(value):
    normal_cdf = 0.5 * (1.0 + lax.erf(value * 0.7071067811865476))
    return normal_cdf + value * jnp.exp(-0.5 * value * value) * 0.3989422804014327


def dot(a, b, contract):
    return lax.dot_general(a, b, (contract, ((), ())), preferred_element_type=F32)


def in_vmem(body, n_scalars, out_shape, operands, flops, scratch=(), limit=SMALL_VMEM):
    spaces = [pltpu.SMEM] * n_scalars + [pltpu.VMEM] * (len(operands) - n_scalars)
    moved = 2 * sum(a.size for a in operands[n_scalars:])
    return pl.pallas_call(
        body,
        in_specs=[pl.BlockSpec(memory_space=space) for space in spaces],
        out_specs=pl.BlockSpec(memory_space=pltpu.VMEM),
        out_shape=jax.ShapeDtypeStruct(out_shape, BF16),
        scratch_shapes=list(scratch),
        compiler_params=pltpu.CompilerParams(vmem_limit_bytes=limit),
        cost_estimate=pl.CostEstimate(flops=flops, bytes_accessed=moved, transcendentals=0),
    )(*operands)


def pick_kernel(slot_ref, arrived_ref, out_ref):
    per_group = arrived_ref.shape[2] // TILE
    for t in range(slot_ref.shape[0]):
        slot = slot_ref[t]
        lanes = pl.multiple_of(lax.rem(slot, per_group) * TILE, TILE)
        out_ref[:, t * TILE : (t + 1) * TILE] = arrived_ref[lax.div(slot, per_group), :, pl.ds(lanes, TILE)]


def proj_kernel(place_ref, mine_ref, other_ref, weight_ref, out_ref):
    half = mine_ref.shape[0]
    core = place_ref[0]
    w_mine = weight_ref[pl.ds(pl.multiple_of(core * half, 16), half), :]
    w_other = weight_ref[pl.ds(pl.multiple_of((1 - core) * half, 16), half), :]
    tiles = mine_ref.shape[1] // TILE
    lows, few = out_ref.shape[0] // tiles, out_ref.shape[1] // 2
    for t in range(tiles):
        tokens = slice(t * TILE, (t + 1) * TILE)
        total = dot(mine_ref[:, tokens], w_mine, ((0,), (0,)))
        total = (total + dot(other_ref[:, tokens], w_other, ((0,), (0,)))).astype(BF16)
        for k in range(2):
            for low in range(lows):
                at = (k * lows + low) * few
                out_ref[t * lows + low, k * few : (k + 1) * few, :] = total[at : at + few]


def final_kernel(place_ref, mine_ref, other_ref, dpre_ref, out_ref, ordered_ref):
    half = mine_ref.shape[0]
    core = place_ref[0]
    tiles = mine_ref.shape[1] // TILE
    lows, few = dpre_ref.shape[0] // tiles, dpre_ref.shape[1] // 2
    for t in range(tiles):
        for k in range(2):
            for low in range(lows):
                at = t * TILE + (k * lows + low) * few
                ordered_ref[at : at + few, :] = dpre_ref[t * lows + low, k * few : (k + 1) * few, :]
    dpre = ordered_ref[...]
    first = pl.ds(pl.multiple_of(core * half, 16), half)
    second = pl.ds(pl.multiple_of((1 - core) * half, 16), half)
    out_ref[first, :] = dot(mine_ref[...], dpre, ((1,), (0,))).astype(BF16)
    out_ref[second, :] = dot(other_ref[...], dpre, ((1,), (0,))).astype(BF16)


def gate_kernel(place_ref, h_hbm, *refs):
    n = (len(refs) - 5) // 4
    weights, out_hbm, held = refs[: 2 * n], refs[2 * n], refs[2 * n + 1 : 4 * n + 1]
    h, turned, out, sems = refs[4 * n + 1 :]
    loads = weight_copies(weights, held, sems)
    load_h = pltpu.make_async_copy(h_hbm, h, sems.at[2 * n])
    load_h.start()
    for i in range(n):
        loads[i].start()
        loads[i + n].start()
    core, blocks, rows = place_ref[0], out.shape[0], out.shape[1]
    _, lows, n_vis, few, width = h.shape
    model = n_vis * width
    load_h.wait()
    for j in range(2):
        slot = core if j == 0 else 1 - core
        for v in range(n_vis):
            block = h[slot, :, v].reshape(lows * few, width)
            at = (j * n_vis + v) * width
            turned[at : at + width, :] = block.astype(F32).T.astype(BF16)
    stores = []
    block, at = 0, 0
    for i in range(n):
        size = held[i].shape[0]
        loads[i].wait()
        loads[i + n].wait()
        total = dot(held[i][...], turned[:model, :], ((1,), (0,)))
        total = total + dot(held[i + n][...], turned[model:, :], ((1,), (0,)))
        out[block, at : at + size, :] = total.astype(BF16)
        at += size
        if at == rows:
            chunk = lax.rem(block + blocks - place_ref[1], blocks)
            stores.append(pltpu.make_async_copy(out.at[block], out_hbm.at[chunk], sems.at[2 * n + 1 + block]))
            stores[-1].start()
            block, at = block + 1, 0
    for store in stores:
        store.wait()


def gate_up(place, hidden, weights, out_shape, flops, turned):
    n = len(weights)
    hbm = pl.BlockSpec(memory_space=pltpu.HBM)
    moved = sum(w.size for w in weights) + hidden.size
    return pl.pallas_call(
        gate_kernel,
        in_specs=[pl.BlockSpec(memory_space=pltpu.SMEM)] + [hbm] * (n + 1),
        out_specs=hbm,
        out_shape=jax.ShapeDtypeStruct(out_shape, BF16),
        scratch_shapes=[pltpu.VMEM(w.shape, BF16) for w in weights]
        + [pltpu.VMEM(hidden.shape, BF16), pltpu.VMEM(turned, BF16), pltpu.VMEM(out_shape, BF16)]
        + [pltpu.SemaphoreType.DMA((n + 1 + out_shape[0],))],
        compiler_params=pltpu.CompilerParams(vmem_limit_bytes=KERNEL_VMEM),
        cost_estimate=pl.CostEstimate(flops=flops, bytes_accessed=2 * moved, transcendentals=0),
    )(place, hidden, *weights)


def dact_body(place_ref, d_ref, weights, out_ref, held, sems, turned):
    n = len(weights) // 2
    copies = weight_copies(weights, held, sems)
    for copy in copies:
        copy.start()
    core, blocks, rows = place_ref[0], d_ref.shape[0], d_ref.shape[1]
    _, lows, n_vis, few, width = out_ref.shape
    for j in range(2):
        for i in range(n):
            copies[j * n + i].wait()
        slot = core if j == 0 else 1 - core
        for v in range(n_vis):
            total, block, at = None, 0, 0
            for i in range(n):
                w = held[j * n + i]
                size = w.shape[0]
                chunk = lax.rem(block + blocks - place_ref[1], blocks)
                term = dot(d_ref[chunk, at : at + size, :], w[:, v * width : (v + 1) * width], ((0,), (0,)))
                total = term if total is None else total + term
                at += size
                block, at = block + at // rows, at % rows
            out_ref[slot, :, v] = total.astype(BF16).reshape(lows, few, width)


def weight_copies(weights, held, sems):
    return [pltpu.make_async_copy(w, b, sems.at[i]) for i, (w, b) in enumerate(zip(weights, held))]


def with_weights(body, place, operand, weights, out_shape, flops, turned, limit):
    n = len(weights)

    def kernel(place_ref, operand_ref, *refs):
        body(place_ref, operand_ref, refs[:n], refs[n], refs[n + 1 : -2], refs[-2], refs[-1])

    moved = sum(w.size for w in weights) + operand.size
    return pl.pallas_call(
        kernel,
        in_specs=[pl.BlockSpec(memory_space=pltpu.SMEM), pl.BlockSpec(memory_space=pltpu.VMEM)]
        + [pl.BlockSpec(memory_space=pltpu.HBM)] * n,
        out_specs=pl.BlockSpec(memory_space=pltpu.VMEM),
        out_shape=jax.ShapeDtypeStruct(out_shape, BF16),
        scratch_shapes=[pltpu.VMEM(w.shape, BF16) for w in weights]
        + [pltpu.SemaphoreType.DMA((n,)), pltpu.VMEM(turned, BF16)],
        compiler_params=pltpu.CompilerParams(vmem_limit_bytes=limit),
        cost_estimate=pl.CostEstimate(flops=flops, bytes_accessed=2 * moved, transcendentals=0),
    )(place, operand, *weights)


def shards(tile_rows, tile_slot, proj_weight, gate_weight, up_weight, cotangent):
    n_vis, n_row, n_col = lax.axis_size("vis"), lax.axis_size("row"), lax.axis_size("col")
    n_x = tile_slot.shape[0]
    n_low = n_row // n_x
    n_quarter = n_col // 2
    row, col, vis = lax.axis_index("row"), lax.axis_index("col"), lax.axis_index("vis")
    core, quarter, x = col % 2, col // 2, row % n_x
    place = jnp.stack([core, vis])
    features = tile_rows.shape[1]
    half = features // 2
    core_pairs = [(2 * i + k, 2 * i + 1 - k) for i in range(n_quarter) for k in range(2)]
    quarter_groups = [[2 * i + k for i in range(n_quarter)] for k in range(2)]
    row_groups = [[low * n_x + i for i in range(n_x) for low in range(n_low)]]
    column_groups = [
        [
            ((low * n_x + i) * n_col + 2 * q + k) * n_vis + v
            for k in range(2)
            for low in range(n_low)
            for v in range(n_vis)
        ]
        for i in range(n_x)
        for q in range(n_quarter)
    ]
    shifts = [0, 1, 3, 2]

    def from_x(value, shift):
        pairs = [
            (low * n_x + i, low * n_x + (i - shift) % n_x) for low in range(n_low) for i in range(n_x)
        ]
        return lax.ppermute(value, "row", pairs)

    def from_core(value):
        return lax.ppermute(value, "col", core_pairs)

    own_half = lax.dynamic_slice_in_dim(tile_rows.T, core * half, half, 0)
    own_half = jnp.broadcast_to(own_half[None], (n_vis,) + own_half.shape)
    arrived = lax.all_to_all(own_half, "vis", 0, 0)
    unit = gate_weight.shape[1]
    pad = -unit % 8
    weights = jnp.stack([gate_weight.T, up_weight.T])
    weights = jnp.pad(weights, ((0, 0), (0, pad), (0, 0))).reshape(2 * (unit + pad), -1)
    right, left, weights_o = from_x(weights, 1), from_x(weights, -1), from_core(weights)
    mine = in_vmem(pick_kernel, 1, (half, n_x * TILE), (tile_slot, arrived), 0, limit=PICK_VMEM)
    other = from_core(mine)

    n_tok, width = n_x * TILE, proj_weight.shape[1]
    share, lane, model = n_tok // n_row, TILE // 2, n_vis * width
    few = share // 2
    flops = 2 * n_tok * features * width
    partial = in_vmem(proj_kernel, 1, (n_row, share, width), (place, mine, other, proj_weight), flops)
    partial, right, left, weights_o = lax.optimization_barrier((partial, right, left, weights_o))
    first = -(weights.shape[0] * 11 // -320) * 16
    far_low, far_high = right[:first], left[first:]
    partial = lax.all_to_all(partial, "row", 0, 0, axis_index_groups=row_groups)
    far_low, far_high = from_x(far_low, 1), from_x(far_high, -1)
    preact = jnp.sum(partial.astype(F32), axis=0)
    hidden = gelu_exact(preact).astype(BF16)
    slope = gelu_slope(preact)

    spread = n_low * n_vis
    hidden = jnp.broadcast_to(hidden.reshape(2, 1, few, width), (2, spread, few, width))
    hidden, far_low, far_high = lax.optimization_barrier((hidden, far_low, far_high))
    hidden = lax.all_to_all(
        hidden.reshape(2 * spread, few, width), ("row", "col", "vis"), 0, 0, axis_index_groups=column_groups
    )
    hidden = hidden.reshape(2, n_low, n_vis, few, width)
    pieces = [weights, right, left, far_low, far_high]
    pieces += [weights_o] + [from_core(w) for w in pieces[1:]]

    offset = (x + n_x - vis) % n_x
    part = sum(jnp.where(offset == shifts[k], k, 0) for k in range(n_x))
    part = (part + n_x - quarter) % n_x
    cot = lax.dynamic_slice(cotangent.T, (part * unit, core * lane), (unit, lane))
    cot_pairs = []
    for low in range(n_low):
        for i in range(n_x):
            for v in range(n_vis):
                for q in range(n_quarter):
                    for k in range(2):
                        there = (low * n_x + (i + shifts[(v + q) % n_x]) % n_x) * n_col + 2 * q + k
                        here = (low * n_x + i) * n_col + 2 * q + k
                        cot_pairs.append((there * n_vis + i, here * n_vis + v))
    cot = lax.ppermute(cot, ("row", "col", "vis"), cot_pairs)
    cot = jnp.pad(cot.astype(F32), ((0, pad), (0, 0)))

    rows = 2 * (unit + pad)
    flops = 4 * lane * n_x * rows * model
    both = gate_up(place, hidden, pieces, (n_x, rows, lane), flops, (2 * model, lane))
    sums = lax.all_to_all(both, "col", 0, 0, axis_index_groups=quarter_groups)
    sums = jnp.sum(sums.astype(F32), axis=0)
    gate_sum, up_sum = sums[: unit + pad], sums[unit + pad :]
    sig = jax.nn.sigmoid(gate_sum)
    d_gate = (cot * up_sum * sig * (1.0 + gate_sum * (1.0 - sig))).astype(BF16)
    d_up = (cot * gate_sum * sig).astype(BF16)
    d_both = jnp.concatenate([d_gate, d_up], axis=0)
    d_all = lax.all_gather(d_both, "col", axis=0, axis_index_groups=quarter_groups)

    shape = (2, n_low, n_vis, few, width)
    dact = with_weights(dact_body, place, d_all, pieces, shape, flops, (16, lane), DACT_VMEM)
    dact = lax.all_to_all(
        dact.reshape(2 * spread, few, width), ("row", "col", "vis"), 0, 0, axis_index_groups=column_groups
    )
    dact = jnp.sum(dact.reshape(2, spread, few, width).astype(F32), axis=1).reshape(share, width)
    dpre = (dact * slope).astype(BF16)
    dpre = lax.all_to_all(
        jnp.broadcast_to(dpre[None], (n_row, share, width)), "row", 0, 0, axis_index_groups=row_groups
    )
    flops = 2 * n_tok * features * width
    return in_vmem(
        final_kernel, 1, (features, width), (place, mine, other, dpre), flops,
        scratch=[pltpu.VMEM((n_tok, width), BF16)],
    )


def solution(mesh):
    in_specs = (
        P("vis", "row"),
        P(),
        P("row", ("col", "vis")),
        P("col", ("row", "vis")),
        P("col", ("row", "vis")),
        P("vis", "row"),
    )
    out_specs = P("row", ("col", "vis"))
    return jax.shard_map(shards, mesh=mesh, in_specs=in_specs, out_specs=out_specs, check_vma=False)
```
